32 devices in a mesh: row: 4 (over z), col: 4 (over y, x), depth: 2 (over core).
Axes of the slice: x: 2, y: 2, z: 4, core: 2. Of those that a mesh axis runs over, the one named last changes fastest.
Arguments:
- right_sides: float32 [24, 32, 128], P('row'), may hold values from -6 to 6
- factor: float32 [24, 24, 128, 128], P('row', ('col', 'depth')), may hold values from -0.21875 to 0.21875
- pattern: int32 [24, 24], P('row', ('col', 'depth')), may hold values 0 or 1
- inverses: float32 [24, 4, 128, 128], P('row'), may hold values from -0.3 to 2.3, as said below
- supernodes: int32 [24], replicated, may hold values from 0 to 8, never falling along the last dimension, each value on 1 to 4 neighbouring positions
- levels: int32 [9], replicated, may hold values from 0 to 2
Outputs:
- solution: float32 [24, 32, 128], P('row')
The draws below stay inside these ranges and needn't reach their ends.
Inputs may be any that keep to these rules, and one draw needn't show every extreme that they name: `inverses`: the tile (p, p) has a diagonal of 0.2 to 2.3. `supernodes`: supernode numbers never fall along the tiles; each supernode holds 1 to 4 consecutive tiles.
All inputs are finite; a program needn't handle non-finite values. No bound on the sum of `pattern` on one device may be relied on, other than what follows from the above.
Results may differ from the reference program's by a relative error of at most 0.0001.
Values sent between devices are 32-bit elements; how exact they have to be, the bound alone decides.
A program may use at most 64 MiB of HBM per device.

```python
import math
import jax
import jax.numpy as jnp
import numpy as np
from jax import lax

B = 128
RHS = 32
MOST = 4
LEVELS = 3
NB = 24
NSUP = 9


def draw_inverses(key, part):
    key = jax.random.fold_in(key, 7)
    noise_key, diag_key = jax.random.split(key)
    shape = (NB, MOST, B, B)
    noise = jnp.clip(jax.random.normal(noise_key, shape, jnp.float32), -6.0, 6.0)
    noise = noise * (0.5 / math.sqrt(B))
    diag_values = jax.random.uniform(diag_key, (NB, 1, B, 1), jnp.float32, 0.5, 2.0)
    on_diag = (lax.broadcasted_iota(jnp.int32, (1, MOST, B, B), 2) == lax.broadcasted_iota(jnp.int32, (1, MOST, B, B), 3)) & (lax.broadcasted_iota(jnp.int32, (1, MOST, B, B), 1) == MOST - 1)
    return noise + jnp.where(on_diag, diag_values, 0.0)


def set_ends(values, own_key, smallest, largest):
    extent = values.shape
    index_at = [jax.random.randint(jax.random.fold_in(own_key, axis), (), 0, extent[axis]) for axis in range(len(extent))]
    values = values.at[tuple(index_at)].set(smallest)
    longest = extent.index(max(extent))
    index_at[longest] = (index_at[longest] + 1) % extent[longest]
    return values.at[tuple(index_at)].set(largest)


def level_of(key, shape, cuts, smallest, high):
    gain = 1.0
    for dim, blocks in cuts:
        steps = jax.random.uniform(jax.random.fold_in(jax.random.fold_in(key, 6), dim), (blocks,), jnp.float32, smallest / len(cuts), high / len(cuts))
        gain = gain * jnp.repeat(jnp.exp(steps), shape[dim] // blocks).reshape((-1,) + (1,) * (len(shape) - 1 - dim))
    return gain


def profile(number_of, total, reach, lean):
    portions = [(1 << 20) // math.isqrt(rank ** lean) + 1 for rank in range(2, number_of + 1)]
    rest, holding = total - reach - (number_of - 1), [1] * (number_of - 1)
    while rest > 0:
        free = [i for i in range(number_of - 1) if holding[i] < reach]
        pool, budget = sum([portions[i] for i in free]), rest
        for i in free:
            addition = min(reach - holding[i], max(1, budget * portions[i] // pool), rest)
            holding[i] = holding[i] + addition
            rest = rest - addition
    return np.array([reach] + holding)


def uneven(own_key, count, total, reach, slope):
    if count == 2:
        one = jax.random.randint(own_key, (), max(1, total - reach), min(reach, total - 1) + 1)
        return jnp.stack([one, total - one])
    lengths = jnp.asarray(profile(count, total, reach, slope), jnp.int32)
    couples = (count - 1) // 2
    giver, sink = lengths[1:1 + 2 * couples:2], lengths[2:2 + 2 * couples:2]
    room = jnp.minimum(giver - 1, reach - sink)
    passed = jax.random.randint(jax.random.fold_in(own_key, 1), (couples,), 0, 1 << 20) % (room + 1)
    lengths = lengths.at[1:1 + 2 * couples:2].set(giver - passed).at[2:2 + 2 * couples:2].set(sink + passed)
    return lengths[jax.random.permutation(jax.random.fold_in(own_key, 2), count)]


def gaussian(stream_key, shape, deviation, most, cuts=(), kind=jnp.bfloat16):
    level = level_of(stream_key, shape, cuts, -0.22, 0.18) if cuts else 1.0
    result = jax.random.normal(stream_key, shape, jnp.float32) * deviation * level
    return jnp.minimum(jnp.maximum(result, -most), most).astype(kind)


def setup_inputs(seed: int = 0) -> dict:
    streams_of = jax.random.split(jax.random.key(seed), 7)
    right_sides = gaussian(streams_of[0], (NB, RHS, B), 1.0, 6.0, ((0, 4),), jnp.float32)
    factor = gaussian(streams_of[1], (NB, NB, B, B), (NB * B // 4) ** -0.5, 0.21875, ((0, 4), (1, 8)), jnp.float32)
    pattern = set_ends((jax.random.randint(streams_of[2], (NB, NB), 0, 2) < 1).astype(jnp.int32), jax.random.fold_in(streams_of[2], 1), 0, 1)
    inverses = draw_inverses(jax.random.fold_in(streams_of[6], 71), 0)
    supernodes = jnp.searchsorted(jnp.cumsum(uneven(streams_of[4], NSUP, NB, MOST, 0)), jnp.arange(NB), side="right").astype(jnp.int32)
    levels = set_ends(jax.random.randint(streams_of[5], (NSUP,), 0, LEVELS), jax.random.fold_in(streams_of[5], 1), 0, LEVELS - 1).astype(jnp.int32)
    return dict(right_sides=right_sides, factor=factor, pattern=pattern, inverses=inverses, supernodes=supernodes, levels=levels)


PREC = lax.Precision.HIGHEST


def lookup(values_table, positions):
    slots = lax.broadcasted_iota(jnp.int32, positions.shape + values_table.shape, positions.ndim)
    picked = jnp.where(positions[..., None] == slots, values_table, 0)
    return jnp.sum(picked, axis=-1).astype(jnp.int32)


def inverse_band(inverses, supernodes, first_tile):
    tile_count, band_tiles, width = inverses.shape[0], inverses.shape[1], inverses.shape[2]
    row_index = first_tile + lax.broadcasted_iota(jnp.int32, (tile_count, band_tiles), 0)
    source = row_index - (band_tiles - 1) + lax.broadcasted_iota(jnp.int32, (tile_count, band_tiles), 1)
    clipped = jnp.clip(source, 0, supernodes.shape[0] - 1).astype(jnp.int32)
    same_node = (source >= 0) & (lookup(supernodes, clipped) == lookup(supernodes, row_index))
    lower_tri = lax.broadcasted_iota(jnp.int32, (width, width), 0) >= lax.broadcasted_iota(jnp.int32, (width, width), 1)
    last_tile = lax.broadcasted_iota(jnp.int32, (band_tiles,), 0) == band_tiles - 1
    inner_mask = jnp.where(last_tile[:, None, None], lower_tri[None], True)
    keep_mask = same_node[:, :, None, None] & inner_mask[None]
    return jnp.where(keep_mask, inverses, 0.0)


def apply_lower(diag_band, padded, tile_count):
    band_tiles = diag_band.shape[1]
    windows = jnp.stack([padded[offset:offset + tile_count] for offset in range(band_tiles)], axis=1)
    return jnp.einsum("pkij,pkrj->pri", diag_band, windows, precision=PREC)


def apply_upper(diag_band, values):
    band_tiles = diag_band.shape[1]
    contrib = jnp.einsum("pkij,pri->pkrj", diag_band, values, precision=PREC)
    pieces = [jnp.pad(contrib[:, offset], ((offset, band_tiles - 1 - offset), (0, 0), (0, 0))) for offset in range(band_tiles)]
    return sum(pieces)


def lower_products(factor, keep_mask, columns):
    def one_row(pieces):
        row_factor, row_keep = pieces
        masked = jnp.where(row_keep[:, None, None], row_factor, 0.0)
        return jnp.einsum("qij,qrj->ri", masked, columns, precision=PREC)
    return lax.map(one_row, (factor, keep_mask))


def upper_products(factor, keep_mask, row_values):
    def add_row(carry, pieces):
        row_factor, row_keep, row_value = pieces
        masked = jnp.where(row_keep[:, None, None], row_factor, 0.0)
        return carry + jnp.einsum("qij,ri->qrj", masked, row_value, precision=PREC), None
    start = jnp.zeros((factor.shape[1],) + row_values.shape[1:], row_values.dtype)
    summed, _ = lax.scan(add_row, start, (factor, keep_mask, row_values))
    return summed


def reference(right_sides, factor, pattern, inverses, supernodes, levels):
    tile_level = lookup(levels, supernodes)
    keep_mask = (tile_level[:, None] > tile_level[None, :]) & (pattern > 0)
    diag_band = inverse_band(inverses, supernodes, 0)
    rim_tiles = MOST - 1
    solved = jnp.zeros_like(right_sides)
    for level_now in range(LEVELS):
        if level_now > 0:
            residual = right_sides - lower_products(factor, keep_mask, solved)
        else:
            residual = right_sides
        padded = jnp.concatenate([jnp.zeros_like(residual[:rim_tiles]), residual], 0)
        update = apply_lower(diag_band, padded, NB)
        solved = jnp.where((tile_level == level_now)[:, None, None], update, solved)
    answer = jnp.zeros_like(right_sides)
    for level_now in range(LEVELS - 1, -1, -1):
        if level_now < LEVELS - 1:
            residual = solved - upper_products(factor, keep_mask, answer)
        else:
            residual = solved
        padded = apply_upper(diag_band, residual)
        answer = jnp.where((tile_level == level_now)[:, None, None], padded[rim_tiles:], answer)
    return answer
```

```python
import functools

import jax
import jax.numpy as jnp
from jax import lax
from jax.experimental import pallas as pl
from jax.experimental.pallas import tpu as pltpu
from jax.sharding import PartitionSpec as P

LEVELS = 3
MESH = pl.DeviceIdType.MESH
F32, BF16 = jnp.float32, jnp.bfloat16
ROWS_BY_ROWS = (((1,), (1,)), ((), ()))
ROWS_BY_COLS = (((1,), (0,)), ((), ()))


def halves(x):
    high = x.astype(BF16).astype(F32)
    return high, x - high


def product(x, w_high, w_low, dims):
    count = x.shape[0]
    stacked = jnp.concatenate(halves(x), axis=0).astype(BF16)
    both = lax.dot_general(stacked, w_high, dims, preferred_element_type=F32)
    both += lax.dot_general(stacked, w_low, dims, preferred_element_type=F32)
    return both[:count] + both[count:]


def kernel(
    rows, cols, depths, rhs_ref, factor_hbm, pattern_ref, inverses_hbm, supernodes_ref, levels_ref,
    out_ref,
    factor_ref, inverses_ref, w_high, w_low, d_high, d_low,
    start_ref, wide_ref, pad_ref, solved_ref, answer_ref,
    send_d, recv_d, send_b, recv_b, send_e, recv_e, send_g, recv_g,
    load_sems, start_sems, d_sems, b_sems, e_sems, g_sems,
):
    row, col, depth = lax.axis_index("row"), lax.axis_index("col"), lax.axis_index("depth")
    group = cols * depths
    place = col * depths + depth
    row_tiles, rhs, width = rhs_ref.shape
    col_tiles = factor_ref.shape[1]
    band = inverses_ref.shape[1]
    chunk = rhs // cols
    span = col_tiles * width
    first, last = row == 0, row == rows - 1
    upper, lower = depth == 1, depth == 0
    home = row == col

    def device(to_row, to_col, to_depth):
        return {"row": to_row, "col": to_col, "depth": to_depth}

    barrier = pltpu.get_barrier_semaphore()
    count = rows * group
    me = row * group + place

    def greet(i, carry):
        to = lax.rem(me + i, count)
        to_place = lax.rem(to, group)
        pl.semaphore_signal(
            barrier, inc=1,
            device_id=device(to // group, to_place // depths, lax.rem(to_place, depths)),
            device_id_type=MESH,
        )
        return carry

    load_inverses = pltpu.make_async_copy(
        inverses_hbm.at[pl.ds(depth * col_tiles, col_tiles)], inverses_ref, load_sems.at[0]
    )
    load_factor = pltpu.make_async_copy(factor_hbm, factor_ref, load_sems.at[1])
    load_inverses.start()
    load_factor.start()
    lax.fori_loop(1, count, greet, 0, unroll=count <= 64)

    def push(src, dst, sems, to):
        pltpu.make_async_remote_copy(
            src_ref=src, dst_ref=dst, send_sem=sems.at[0], recv_sem=sems.at[1],
            device_id=to, device_id_type=MESH,
        ).start()

    def await_units(ruler, sem, cases):
        for condition, units in cases:
            if units:

                @pl.when(condition)
                def _(units=units):
                    part = ruler.at[pl.ds(0, units)]
                    pltpu.make_async_copy(part, part, sem).wait()

    def level_of(tile):
        return levels_ref[supernodes_ref[tile]]

    def lanes(scalars):
        return jnp.concatenate([jnp.full((1, width), s, F32) for s in scalars], axis=1)

    one, zero = jnp.float32(1), jnp.float32(0)

    for p in range(row_tiles):
        half, t = divmod(p, col_tiles)
        piece = rhs_ref[p, pl.ds(pl.multiple_of(col * chunk, chunk), chunk), :]

        @pl.when(depth == half)
        def _(t=t, piece=piece):
            start_ref[1, :, t * width : (t + 1) * width] = piece

        if half == 0:

            @pl.when(upper)
            def _(t=t, piece=piece):
                start_ref[0, :, t * width : (t + 1) * width] = piece

    @pl.when(lower & first)
    def _():
        start_ref[0] = jnp.zeros((chunk, span), F32)

    pl.semaphore_wait(barrier, count - 1)

    @pl.when(upper & jnp.logical_not(last))
    def _():
        push(start_ref.at[1], start_ref.at[0], start_sems, device(row + 1, col, 0))

    load_inverses.wait()
    own_first = row * row_tiles + depth * col_tiles
    own_level = [level_of(own_first + t) for t in range(col_tiles)]
    under = lax.broadcasted_iota(jnp.int32, (width, width), 0) >= lax.broadcasted_iota(
        jnp.int32, (width, width), 1
    )
    for t in range(col_tiles):
        tile = own_first + t
        for k in range(band):
            source = tile - (band - 1) + k
            if k == band - 1:
                kept = jnp.where(under, inverses_ref[t, k], 0.0)
            else:
                same = (source >= 0) & (
                    supernodes_ref[jnp.maximum(source, 0)] == supernodes_ref[tile]
                )
                kept = inverses_ref[t, k] * jnp.where(same, one, zero)
            high, low = halves(kept)
            d_high[t, :, k * width : (k + 1) * width] = high.astype(BF16)
            d_low[t, :, k * width : (k + 1) * width] = low.astype(BF16)

    @pl.when(lower & jnp.logical_not(first))
    def _():
        pltpu.make_async_copy(start_ref.at[0], start_ref.at[0], start_sems.at[1]).wait()

    own_mask = [
        lanes([jnp.where(v == level, one, zero) for v in own_level]) for level in range(LEVELS)
    ]

    def widen(value):
        if chunk >= 8:
            return value
        pad_ref[...] = jnp.zeros_like(pad_ref)
        pad_ref[0:chunk, 0 : value.shape[1]] = value
        return pad_ref[:, 0 : value.shape[1]]

    def solve_own(level, residual):
        x = widen(residual)
        update = jnp.concatenate(
            [
                product(
                    x[:, t * width : (t + band) * width], d_high[t], d_low[t], ROWS_BY_ROWS
                )
                for t in range(col_tiles)
            ],
            axis=1,
        )[:chunk]
        now = update * own_mask[level]
        solved_ref[...] = now if level == 0 else solved_ref[...] + now

    def spread_solved(level):
        send_d[level] = solved_ref[...]
        for to in range(rows):

            @pl.when(jnp.logical_not(home & (row == to)))
            def _(to=to):
                push(send_d.at[level], recv_d.at[level, col], d_sems.at[level], device(to, row, depth))

        @pl.when(home)
        def _():
            recv_d[level, col] = solved_ref[...]

    def start_vector():
        return jnp.concatenate([start_ref[0], start_ref[1]], axis=1)

    solve_own(0, start_vector())
    spread_solved(0)

    load_factor.wait()
    row_level = [level_of(row * row_tiles + p) for p in range(row_tiles)]
    col_level = [level_of(place * col_tiles + q) for q in range(col_tiles)]
    for p in range(row_tiles):
        for q in range(col_tiles):
            keep = (row_level[p] > col_level[q]) & (pattern_ref[p, q] > 0)
            high, low = halves(factor_ref[p, q] * jnp.where(keep, one, zero))
            at = (slice(p * width, (p + 1) * width), slice(q * width, (q + 1) * width))
            w_high[at] = high.astype(BF16)
            w_low[at] = low.astype(BF16)
    row_mask = [
        lanes([jnp.where(v == level, one, zero) for v in row_level]) for level in range(LEVELS)
    ]

    column_cases = [(jnp.logical_not(home), rows), (home, rows - 1)]

    def reduce_rows(level):
        await_units(recv_d.at[level], d_sems.at[level, 1], column_cases)
        for k in range(cols):
            wide_ref[k * chunk : (k + 1) * chunk, 0:span] = recv_d[level, k]
        wide_ref[...] = product(wide_ref[:, 0:span], w_high[...], w_low[...], ROWS_BY_ROWS)
        for k in range(cols):
            for half in range(2):
                send_b[level, k, half] = wide_ref[
                    k * chunk : (k + 1) * chunk, half * span : (half + 1) * span
                ]
        src, dst, sems = send_b.at[level], recv_b.at[level], b_sems.at[level]

        for step in range(1, group):
            to = lax.rem(place + step, group)
            to_col, to_depth = to // depths, lax.rem(to, depths)
            slot = group - step

            @pl.when(to_depth == 1)
            def _(to_col=to_col, slot=slot):
                push(
                    src.at[to_col], dst.at[pl.ds(2 * slot, 2)], sems, device(row, to_col, 1)
                )

            @pl.when(to_depth == 0)
            def _(to_col=to_col, slot=slot):
                push(
                    src.at[to_col, 0], dst.at[2 * slot + 1], sems, device(row, to_col, 0)
                )

        @pl.when(jnp.logical_not(last))
        def _():
            for k in range(cols):
                slot = lax.rem(place - k * depths + group, group)
                push(src.at[k, 1], dst.at[2 * slot], sems, device(row + 1, k, 0))

        recv_b[level, 1] = send_b[level, col, depth]

        @pl.when(upper)
        def _():
            recv_b[level, 0] = send_b[level, col, 0]

        @pl.when(lower & first)
        def _():
            for slot in range(group):
                recv_b[level, 2 * slot] = jnp.zeros((chunk, span), F32)

        await_units(
            dst, sems.at[1],
            [
                (upper, 2 * (group - 1)),
                (lower & first, group - 1),
                (lower & jnp.logical_not(first), 2 * group - 1),
            ],
        )
        sums = []
        for part in range(2):
            total = recv_b[level, part]
            for slot in range(1, group):
                total += recv_b[level, 2 * slot + part]
            sums.append(total)
        return jnp.concatenate(sums, axis=1)

    for level in range(1, LEVELS):
        solve_own(level, start_vector() - reduce_rows(level - 1))
        if level + 1 < LEVELS:
            spread_solved(level)

    gather_sends = [
        (upper, 2 * (group - 1)),
        (lower & first, group - 1),
        (lower & jnp.logical_not(first), 2 * group - 1),
    ]
    whole = cols + 2 * cols
    gather_receives = [
        (upper & last, whole - 2),
        (lower & last, whole - 1),
        (upper & jnp.logical_not(last), whole - 2 + cols),
        (lower & jnp.logical_not(last), whole - 1 + cols),
    ]

    def spread_answer(step, residual):
        x = widen(residual)
        pieces = [None] * (2 * col_tiles)
        for t in range(col_tiles):
            given = product(
                x[:, t * width : (t + 1) * width], d_high[t], d_low[t], ROWS_BY_COLS
            )
            for k in range(band):
                piece = given[:chunk, k * width : (k + 1) * width]
                u = t + k - (band - 1) + col_tiles
                pieces[u] = piece if pieces[u] is None else pieces[u] + piece
        for u, piece in enumerate(pieces):
            half, t = divmod(u, col_tiles)
            send_e[step, half, :, t * width : (t + 1) * width] = (
                jnp.zeros((chunk, width), F32) if piece is None else piece
            )
        src, dst, sems = send_e.at[step], recv_e.at[step], e_sems.at[step]

        @pl.when(upper)
        def _():
            for other in range(1, group):
                to = lax.rem(place + other, group)
                push(
                    src, dst.at[pl.ds(2 * col, 2)], sems,
                    device(row, to // depths, lax.rem(to, depths)),
                )
            recv_e[step, pl.ds(2 * col, 2)] = send_e[step]

        @pl.when(lower)
        def _():
            for other in range(1, group):
                to = lax.rem(place + other, group)
                push(
                    src.at[1], dst.at[2 * cols + 2 * col], sems,
                    device(row, to // depths, lax.rem(to, depths)),
                )
            recv_e[step, 2 * cols + 2 * col] = send_e[step, 1]

        @pl.when(lower & jnp.logical_not(first))
        def _():
            for to in range(group):
                push(
                    src.at[0], dst.at[2 * cols + 2 * col + 1], sems,
                    device(row - 1, to // depths, to % depths),
                )

        @pl.when(last)
        def _():
            for k in range(cols):
                recv_e[step, 2 * cols + 2 * k + 1] = jnp.zeros((chunk, span), F32)

        await_units(dst, sems.at[1], gather_receives)
        mask = row_mask[LEVELS - 1 - step]
        for k in range(cols):
            for half in range(2):
                at = (slice(k * chunk, (k + 1) * chunk), slice(half * span, (half + 1) * span))
                now = recv_e[step, 2 * k + half] + recv_e[step, 2 * cols + 2 * k + half]
                now = now * mask[:, half * span : (half + 1) * span]
                answer_ref[at] = now if step == 0 else answer_ref[at] + now

    def column_sums(step):
        wide_ref[:, 0:span] = product(answer_ref[...], w_high[...], w_low[...], ROWS_BY_COLS)
        for k in range(cols):
            send_g[step, k] = wide_ref[k * chunk : (k + 1) * chunk, 0:span]
        for k in range(cols):

            @pl.when(jnp.logical_not(home & (col == k)))
            def _(k=k):
                push(
                    send_g.at[step, k], recv_g.at[step, row], g_sems.at[step], device(col, k, depth)
                )

        @pl.when(home)
        def _():
            recv_g[step, row] = send_g[step, col]

        await_units(recv_g.at[step], g_sems.at[step, 1], column_cases)
        total = recv_g[step, 0]
        for r in range(1, rows):
            total += recv_g[step, r]
        return total

    spread_answer(0, solved_ref[...])
    for step in range(1, LEVELS):
        spread_answer(step, solved_ref[...] - column_sums(step - 1))

    for p in range(row_tiles):
        out_ref[p] = answer_ref[:, p * width : (p + 1) * width]

    @pl.when(upper & jnp.logical_not(last))
    def _():
        pltpu.make_async_copy(start_ref.at[1], start_ref.at[1], start_sems.at[0]).wait()

    reduce_sends = [
        (upper & last, whole - 2),
        (lower & last, whole - 1),
        (upper & jnp.logical_not(last), whole - 2 + cols),
        (lower & jnp.logical_not(last), whole - 1 + cols),
    ]
    for level in range(LEVELS - 1):
        await_units(recv_d.at[level], d_sems.at[level, 0], column_cases)
        await_units(recv_b.at[level], b_sems.at[level, 0], reduce_sends)
        await_units(recv_g.at[level], g_sems.at[level, 0], column_cases)
    for step in range(LEVELS):
        await_units(recv_e.at[step], e_sems.at[step, 0], gather_sends)


def shards(rows, cols, depths, right_sides, factor, pattern, inverses, supernodes, levels):
    row_tiles, rhs, width = right_sides.shape
    col_tiles, band = factor.shape[1], inverses.shape[1]
    group = cols * depths
    assert depths == 2 and rows == cols and row_tiles == depths * col_tiles
    assert rhs % cols == 0 and band - 1 <= col_tiles
    chunk, span = rhs // cols, col_tiles * width
    unit = (chunk, span)
    vmem = pl.BlockSpec(memory_space=pltpu.VMEM)
    smem = pl.BlockSpec(memory_space=pltpu.SMEM)
    hbm = pl.BlockSpec(memory_space=pl.ANY)
    steps = LEVELS - 1
    dma = pltpu.SemaphoreType.DMA
    return pl.pallas_call(
        functools.partial(kernel, rows, cols, depths),
        out_shape=jax.ShapeDtypeStruct(right_sides.shape, F32),
        in_specs=[vmem, hbm, smem, hbm, smem, smem],
        out_specs=vmem,
        scratch_shapes=[
            pltpu.VMEM(factor.shape, F32),
            pltpu.VMEM((col_tiles,) + inverses.shape[1:], F32),
            pltpu.VMEM((row_tiles * width, span), BF16),
            pltpu.VMEM((row_tiles * width, span), BF16),
            pltpu.VMEM((col_tiles, width, band * width), BF16),
            pltpu.VMEM((col_tiles, width, band * width), BF16),
            pltpu.VMEM((2,) + unit, F32),
            pltpu.VMEM((rhs, row_tiles * width), F32),
            pltpu.VMEM((8, row_tiles * width), F32),
            pltpu.VMEM(unit, F32),
            pltpu.VMEM((rhs, row_tiles * width), F32),
            pltpu.VMEM((steps,) + unit, F32),
            pltpu.VMEM((steps, cols) + unit, F32),
            pltpu.VMEM((steps, cols, 2) + unit, F32),
            pltpu.VMEM((steps, 2 * group) + unit, F32),
            pltpu.VMEM((LEVELS, 2) + unit, F32),
            pltpu.VMEM((LEVELS, 4 * cols) + unit, F32),
            pltpu.VMEM((steps, cols) + unit, F32),
            pltpu.VMEM((steps, rows) + unit, F32),
            dma((2,)),
            dma((2,)),
            dma((steps, 2)),
            dma((steps, 2)),
            dma((LEVELS, 2)),
            dma((steps, 2)),
        ],
        compiler_params=pltpu.CompilerParams(
            collective_id=0, has_side_effects=True, vmem_limit_bytes=32 * 1024 * 1024
        ),
    )(right_sides, factor, pattern, inverses, supernodes, levels)


def solution(mesh):
    rows, cols, depths = (mesh.shape[axis] for axis in ("row", "col", "depth"))
    return jax.shard_map(
        functools.partial(shards, rows, cols, depths),
        mesh=mesh,
        in_specs=(
            P("row", None, None),
            P("row", ("col", "depth"), None, None),
            P("row", ("col", "depth")),
            P("row", None, None, None),
            P(),
            P(),
        ),
        out_specs=P("row", None, None),
        check_vma=False,
    )
```

```python
import functools

import jax
import jax.numpy as jnp
from jax import lax
from jax.experimental import pallas as pl
from jax.experimental.pallas import tpu as pltpu
from jax.sharding import PartitionSpec as P

LEVELS = 3
MESH = pl.DeviceIdType.MESH
F32, BF16 = jnp.float32, jnp.bfloat16
ROWS_BY_ROWS = (((1,), (1,)), ((), ()))
ROWS_BY_COLS = (((1,), (0,)), ((), ()))


def halves(x):
    high = x.astype(BF16).astype(F32)
    return high, x - high


def product(x, w_high, w_low, dims):
    count = x.shape[0]
    stacked = jnp.concatenate(halves(x), axis=0).astype(BF16)
    both = lax.dot_general(stacked, w_high, dims, preferred_element_type=F32)
    both += lax.dot_general(stacked, w_low, dims, preferred_element_type=F32)
    return both[:count] + both[count:]


def kernel(
    rows, cols, depths, rhs_hbm, factor_hbm, pattern_hbm, inverses_hbm, supernodes_hbm, levels_hbm,
    out_ref,
    rhs_ref, pattern_ref, supernodes_ref, levels_ref, factor_ref, inverses_ref, w_high, w_low, d_high, d_low,
    start_ref, wide_ref, pad_ref, solved_ref, answer_ref,
    send_d, recv_d, send_b, recv_b, send_e, recv_e, send_g, recv_g,
    load_sems, start_sems, d_sems, b_sems, e_sems, g_sems,
):
    row, col, depth = lax.axis_index("row"), lax.axis_index("col"), lax.axis_index("depth")
    group = cols * depths
    place = col * depths + depth
    row_tiles, rhs, width = rhs_ref.shape
    col_tiles = factor_ref.shape[1]
    band = inverses_ref.shape[1]
    chunk = rhs // cols
    span = col_tiles * width
    first, last = row == 0, row == rows - 1
    upper, lower = depth == 1, depth == 0
    home = row == col

    def device(to_row, to_col, to_depth):
        return {"row": to_row, "col": to_col, "depth": to_depth}

    barrier = pltpu.get_barrier_semaphore()
    count = rows * group
    me = row * group + place

    def greet(i, carry):
        to = lax.rem(me + i, count)
        to_place = lax.rem(to, group)
        pl.semaphore_signal(
            barrier, inc=1,
            device_id=device(to // group, to_place // depths, lax.rem(to_place, depths)),
            device_id_type=MESH,
        )
        return carry

    load_inverses = pltpu.make_async_copy(
        inverses_hbm.at[pl.ds(depth * col_tiles, col_tiles)], inverses_ref, load_sems.at[0]
    )
    load_factor = pltpu.make_async_copy(factor_hbm, factor_ref, load_sems.at[1])
    small_loads = [
        pltpu.make_async_copy(src, dst, load_sems.at[2 + i])
        for i, (src, dst) in enumerate(
            [
                (rhs_hbm, rhs_ref),
                (supernodes_hbm, supernodes_ref),
                (levels_hbm, levels_ref),
                (pattern_hbm, pattern_ref),
            ]
        )
    ]
    for load in small_loads:
        load.start()
    load_inverses.start()
    load_factor.start()
    lax.fori_loop(1, count, greet, 0, unroll=count <= 64)
    for load in small_loads:
        load.wait()

    def push(src, dst, sems, to):
        pltpu.make_async_remote_copy(
            src_ref=src, dst_ref=dst, send_sem=sems.at[0], recv_sem=sems.at[1],
            device_id=to, device_id_type=MESH,
        ).start()

    def await_units(ruler, sem, cases):
        for condition, units in cases:
            if units:

                @pl.when(condition)
                def _(units=units):
                    part = ruler.at[pl.ds(0, units)]
                    pltpu.make_async_copy(part, part, sem).wait()

    def level_of(tile):
        return levels_ref[supernodes_ref[tile]]

    def lanes(scalars):
        return jnp.concatenate([jnp.full((1, width), s, F32) for s in scalars], axis=1)

    one, zero = jnp.float32(1), jnp.float32(0)

    for p in range(row_tiles):
        half, t = divmod(p, col_tiles)
        piece = rhs_ref[p, pl.ds(pl.multiple_of(col * chunk, chunk), chunk), :]

        @pl.when(depth == half)
        def _(t=t, piece=piece):
            start_ref[1, :, t * width : (t + 1) * width] = piece

        if half == 0:

            @pl.when(upper)
            def _(t=t, piece=piece):
                start_ref[0, :, t * width : (t + 1) * width] = piece

    @pl.when(lower & first)
    def _():
        start_ref[0] = jnp.zeros((chunk, span), F32)

    load_inverses.wait()
    own_first = row * row_tiles + depth * col_tiles
    own_level = [level_of(own_first + t) for t in range(col_tiles)]
    under = lax.broadcasted_iota(jnp.int32, (width, width), 0) >= lax.broadcasted_iota(
        jnp.int32, (width, width), 1
    )
    for t in range(col_tiles):
        tile = own_first + t
        for k in range(band):
            source = tile - (band - 1) + k
            if k == band - 1:
                kept = jnp.where(under, inverses_ref[t, k], 0.0)
            else:
                same = (source >= 0) & (
                    supernodes_ref[jnp.maximum(source, 0)] == supernodes_ref[tile]
                )
                kept = inverses_ref[t, k] * jnp.where(same, one, zero)
            high, low = halves(kept)
            d_high[t, :, k * width : (k + 1) * width] = high.astype(BF16)
            d_low[t, :, k * width : (k + 1) * width] = low.astype(BF16)

    load_factor.wait()
    row_level = [level_of(row * row_tiles + p) for p in range(row_tiles)]
    col_level = [level_of(place * col_tiles + q) for q in range(col_tiles)]
    for p in range(row_tiles):
        for q in range(col_tiles):
            keep = (row_level[p] > col_level[q]) & (pattern_ref[q, p] > 0)
            high, low = halves(factor_ref[p, q] * jnp.where(keep, one, zero))
            at = (slice(p * width, (p + 1) * width), slice(q * width, (q + 1) * width))
            w_high[at] = high.astype(BF16)
            w_low[at] = low.astype(BF16)
    row_mask = [
        lanes([jnp.where(v == level, one, zero) for v in row_level]) for level in range(LEVELS)
    ]

    pl.semaphore_wait(barrier, count - 1)

    @pl.when(upper & jnp.logical_not(last))
    def _():
        push(start_ref.at[1], start_ref.at[0], start_sems, device(row + 1, col, 0))

    @pl.when(lower & jnp.logical_not(first))
    def _():
        pltpu.make_async_copy(start_ref.at[0], start_ref.at[0], start_sems.at[1]).wait()

    own_mask = [
        lanes([jnp.where(v == level, one, zero) for v in own_level]) for level in range(LEVELS)
    ]

    def widen(value):
        if chunk >= 8:
            return value
        pad_ref[...] = jnp.zeros_like(pad_ref)
        pad_ref[0:chunk, 0 : value.shape[1]] = value
        return pad_ref[:, 0 : value.shape[1]]

    def solve_own(level, residual):
        x = widen(residual)
        update = jnp.concatenate(
            [
                product(
                    x[:, t * width : (t + band) * width], d_high[t], d_low[t], ROWS_BY_ROWS
                )
                for t in range(col_tiles)
            ],
            axis=1,
        )[:chunk]
        now = update * own_mask[level]
        solved_ref[...] = now if level == 0 else solved_ref[...] + now

    def spread_solved(level):
        send_d[level] = solved_ref[...]
        for to in range(rows):

            @pl.when(jnp.logical_not(home & (row == to)))
            def _(to=to):
                push(send_d.at[level], recv_d.at[level, col], d_sems.at[level], device(to, row, depth))

        @pl.when(home)
        def _():
            recv_d[level, col] = solved_ref[...]

    def start_vector():
        return jnp.concatenate([start_ref[0], start_ref[1]], axis=1)

    solve_own(0, start_vector())
    spread_solved(0)

    column_cases = [(jnp.logical_not(home), rows), (home, rows - 1)]

    def reduce_rows(level):
        await_units(recv_d.at[level], d_sems.at[level, 1], column_cases)
        for k in range(cols):
            wide_ref[k * chunk : (k + 1) * chunk, 0:span] = recv_d[level, k]
        wide_ref[...] = product(wide_ref[:, 0:span], w_high[...], w_low[...], ROWS_BY_ROWS)
        for k in range(cols):
            for half in range(2):
                send_b[level, k, half] = wide_ref[
                    k * chunk : (k + 1) * chunk, half * span : (half + 1) * span
                ]
        src, dst, sems = send_b.at[level], recv_b.at[level], b_sems.at[level]

        for step in range(1, group):
            to = lax.rem(place + step, group)
            to_col, to_depth = to // depths, lax.rem(to, depths)
            slot = group - step

            @pl.when(to_depth == 1)
            def _(to_col=to_col, slot=slot):
                push(
                    src.at[to_col], dst.at[pl.ds(2 * slot, 2)], sems, device(row, to_col, 1)
                )

            @pl.when(to_depth == 0)
            def _(to_col=to_col, slot=slot):
                push(
                    src.at[to_col, 0], dst.at[2 * slot + 1], sems, device(row, to_col, 0)
                )

        @pl.when(jnp.logical_not(last))
        def _():
            for k in range(cols):
                slot = lax.rem(place - k * depths + group, group)
                push(src.at[k, 1], dst.at[2 * slot], sems, device(row + 1, k, 0))

        recv_b[level, 1] = send_b[level, col, depth]

        @pl.when(upper)
        def _():
            recv_b[level, 0] = send_b[level, col, 0]

        @pl.when(lower & first)
        def _():
            for slot in range(group):
                recv_b[level, 2 * slot] = jnp.zeros((chunk, span), F32)

        await_units(
            dst, sems.at[1],
            [
                (upper, 2 * (group - 1)),
                (lower & first, group - 1),
                (lower & jnp.logical_not(first), 2 * group - 1),
            ],
        )
        sums = []
        for part in range(2):
            total = recv_b[level, part]
            for slot in range(1, group):
                total += recv_b[level, 2 * slot + part]
            sums.append(total)
        return jnp.concatenate(sums, axis=1)

    for level in range(1, LEVELS):
        solve_own(level, start_vector() - reduce_rows(level - 1))
        if level + 1 < LEVELS:
            spread_solved(level)

    gather_sends = [
        (upper, 2 * (group - 1)),
        (lower & first, group - 1),
        (lower & jnp.logical_not(first), 2 * group - 1),
    ]
    whole = cols + 2 * cols
    gather_receives = [
        (upper & last, whole - 2),
        (lower & last, whole - 1),
        (upper & jnp.logical_not(last), whole - 2 + cols),
        (lower & jnp.logical_not(last), whole - 1 + cols),
    ]

    def spread_answer(step, residual):
        x = widen(residual)
        pieces = [None] * (2 * col_tiles)
        for t in range(col_tiles):
            given = product(
                x[:, t * width : (t + 1) * width], d_high[t], d_low[t], ROWS_BY_COLS
            )
            for k in range(band):
                piece = given[:chunk, k * width : (k + 1) * width]
                u = t + k - (band - 1) + col_tiles
                pieces[u] = piece if pieces[u] is None else pieces[u] + piece
        for u, piece in enumerate(pieces):
            half, t = divmod(u, col_tiles)
            send_e[step, half, :, t * width : (t + 1) * width] = (
                jnp.zeros((chunk, width), F32) if piece is None else piece
            )
        src, dst, sems = send_e.at[step], recv_e.at[step], e_sems.at[step]

        @pl.when(upper)
        def _():
            for other in range(1, group):
                to = lax.rem(place + other, group)
                push(
                    src, dst.at[pl.ds(2 * col, 2)], sems,
                    device(row, to // depths, lax.rem(to, depths)),
                )
            recv_e[step, pl.ds(2 * col, 2)] = send_e[step]

        @pl.when(lower)
        def _():
            for other in range(1, group):
                to = lax.rem(place + other, group)
                push(
                    src.at[1], dst.at[2 * cols + 2 * col], sems,
                    device(row, to // depths, lax.rem(to, depths)),
                )
            recv_e[step, 2 * cols + 2 * col] = send_e[step, 1]

        @pl.when(lower & jnp.logical_not(first))
        def _():
            for to in range(group):
                push(
                    src.at[0], dst.at[2 * cols + 2 * col + 1], sems,
                    device(row - 1, to // depths, to % depths),
                )

        @pl.when(last)
        def _():
            for k in range(cols):
                recv_e[step, 2 * cols + 2 * k + 1] = jnp.zeros((chunk, span), F32)

        await_units(dst, sems.at[1], gather_receives)
        mask = row_mask[LEVELS - 1 - step]
        for k in range(cols):
            for half in range(2):
                at = (slice(k * chunk, (k + 1) * chunk), slice(half * span, (half + 1) * span))
                now = recv_e[step, 2 * k + half] + recv_e[step, 2 * cols + 2 * k + half]
                now = now * mask[:, half * span : (half + 1) * span]
                answer_ref[at] = now if step == 0 else answer_ref[at] + now

    def column_sums(step):
        wide_ref[:, 0:span] = product(answer_ref[...], w_high[...], w_low[...], ROWS_BY_COLS)
        for k in range(cols):
            send_g[step, k] = wide_ref[k * chunk : (k + 1) * chunk, 0:span]
        for k in range(cols):

            @pl.when(jnp.logical_not(home & (col == k)))
            def _(k=k):
                push(
                    send_g.at[step, k], recv_g.at[step, row], g_sems.at[step], device(col, k, depth)
                )

        @pl.when(home)
        def _():
            recv_g[step, row] = send_g[step, col]

        await_units(recv_g.at[step], g_sems.at[step, 1], column_cases)
        total = recv_g[step, 0]
        for r in range(1, rows):
            total += recv_g[step, r]
        return total

    spread_answer(0, solved_ref[...])
    for step in range(1, LEVELS):
        spread_answer(step, solved_ref[...] - column_sums(step - 1))

    for p in range(row_tiles):
        out_ref[p] = answer_ref[:, p * width : (p + 1) * width]

    @pl.when(upper & jnp.logical_not(last))
    def _():
        pltpu.make_async_copy(start_ref.at[1], start_ref.at[1], start_sems.at[0]).wait()

    reduce_sends = [
        (upper & last, whole - 2),
        (lower & last, whole - 1),
        (upper & jnp.logical_not(last), whole - 2 + cols),
        (lower & jnp.logical_not(last), whole - 1 + cols),
    ]
    for level in range(LEVELS - 1):
        await_units(recv_d.at[level], d_sems.at[level, 0], column_cases)
        await_units(recv_b.at[level], b_sems.at[level, 0], reduce_sends)
        await_units(recv_g.at[level], g_sems.at[level, 0], column_cases)
    for step in range(LEVELS):
        await_units(recv_e.at[step], e_sems.at[step, 0], gather_sends)


def shards(rows, cols, depths, right_sides, factor, pattern, inverses, supernodes, levels):
    row_tiles, rhs, width = right_sides.shape
    col_tiles, band = factor.shape[1], inverses.shape[1]
    group = cols * depths
    assert depths == 2 and rows == cols and row_tiles == depths * col_tiles
    assert rhs % cols == 0 and band - 1 <= col_tiles
    chunk, span = rhs // cols, col_tiles * width
    unit = (chunk, span)
    vmem = pl.BlockSpec(memory_space=pltpu.VMEM)
    hbm = pl.BlockSpec(memory_space=pltpu.HBM)
    steps = LEVELS - 1
    dma = pltpu.SemaphoreType.DMA
    return pl.pallas_call(
        functools.partial(kernel, rows, cols, depths),
        out_shape=jax.ShapeDtypeStruct(right_sides.shape, F32),
        in_specs=[hbm] * 6,
        out_specs=vmem,
        scratch_shapes=[
            pltpu.VMEM(right_sides.shape, F32),
            pltpu.SMEM(pattern.shape[::-1], jnp.int32),
            pltpu.SMEM(supernodes.shape, jnp.int32),
            pltpu.SMEM(levels.shape, jnp.int32),
            pltpu.VMEM(factor.shape, F32),
            pltpu.VMEM((col_tiles,) + inverses.shape[1:], F32),
            pltpu.VMEM((row_tiles * width, span), BF16),
            pltpu.VMEM((row_tiles * width, span), BF16),
            pltpu.VMEM((col_tiles, width, band * width), BF16),
            pltpu.VMEM((col_tiles, width, band * width), BF16),
            pltpu.VMEM((2,) + unit, F32),
            pltpu.VMEM((rhs, row_tiles * width), F32),
            pltpu.VMEM((8, row_tiles * width), F32),
            pltpu.VMEM(unit, F32),
            pltpu.VMEM((rhs, row_tiles * width), F32),
            pltpu.VMEM((steps,) + unit, F32),
            pltpu.VMEM((steps, cols) + unit, F32),
            pltpu.VMEM((steps, cols, 2) + unit, F32),
            pltpu.VMEM((steps, 2 * group) + unit, F32),
            pltpu.VMEM((LEVELS, 2) + unit, F32),
            pltpu.VMEM((LEVELS, 4 * cols) + unit, F32),
            pltpu.VMEM((steps, cols) + unit, F32),
            pltpu.VMEM((steps, rows) + unit, F32),
            dma((6,)),
            dma((2,)),
            dma((steps, 2)),
            dma((steps, 2)),
            dma((LEVELS, 2)),
            dma((steps, 2)),
        ],
        compiler_params=pltpu.CompilerParams(
            collective_id=0, has_side_effects=True, vmem_limit_bytes=60 * 1024 * 1024
        ),
    )(right_sides, factor, pattern.T, inverses, supernodes, levels)


def solution(mesh):
    rows, cols, depths = (mesh.shape[axis] for axis in ("row", "col", "depth"))
    return jax.shard_map(
        functools.partial(shards, rows, cols, depths),
        mesh=mesh,
        in_specs=(
            P("row", None, None),
            P("row", ("col", "depth"), None, None),
            P("row", ("col", "depth")),
            P("row", None, None, None),
            P(),
            P(),
        ),
        out_specs=P("row", None, None),
        check_vma=False,
    )
```
